32 devices in a mesh: lat: 8 (over z, x), lon: 4 (over y, core).
Axes of the slice: x: 2, y: 2, z: 4, core: 2. Of those that a mesh axis runs over, the one named last changes fastest.
Arguments:
- zonal_wind: float32 [64, 72, 2880], P('lat', None, 'lon'), may hold values from -6 to 6
- merid_wind: float32 [64, 72, 2880], P('lat', None, 'lon'), may hold values from -6 to 6
- pressure: float32 [64, 72, 2880], P('lat', None, 'lon'), may hold values from -6 to 6
- zonal_metric: float32 [64], P('lat'), may hold values from 0.2 to 1
- helm_inverse: float32 [64, 72, 72], P('lat'), may hold values from -0.06 to 1.06
- kernel_taps: float32 [16, 512], replicated, may hold values from 0.05 to 1
- filter_width: int32 [16], replicated, may hold values from 16 to 256
Outputs:
- zonal_out: float32 [64, 72, 2880], P('lat', None, 'lon')
- merid_out: float32 [64, 72, 2880], P('lat', None, 'lon')
- pressure_out: float32 [64, 72, 2880], P('lat', None, 'lon')
The draws below stay inside these ranges and needn't reach their ends.
All inputs are finite; a program needn't handle non-finite values.
Results may differ from the reference program's by a relative error of at most 0.0001.
Values sent between devices are 32-bit elements; how exact they have to be, the bound alone decides.
A program may use at most 128 MiB of HBM per device.

```python
import math
import jax
import jax.numpy as jnp
from jax import lax

ROWS = 8
LEV = 72
LON = 2880
KW = 512
HALF = 256
NLAT = 64


def draw_helm_inverse(key, part):
    array_shape = (NLAT, LEV, LEV)
    noise = jax.random.uniform(key, array_shape, jnp.float32, -0.06, 0.06)
    return jnp.eye(LEV, dtype=jnp.float32)[None] + noise


def plant(drawn, own_key, smallest, high):
    dims = drawn.shape
    place = [jax.random.randint(jax.random.fold_in(own_key, axis), (), 0, dims[axis]) for axis in range(len(dims))]
    drawn = drawn.at[tuple(place)].set(smallest)
    longest = dims.index(max(dims))
    place[longest] = (place[longest] + 1) % dims[longest]
    return drawn.at[tuple(place)].set(high)


def steps_of(key, shape, split, smallest, top_value):
    gain, own = 1.0, jax.random.fold_in(key, 6)
    for axis_at, blocks in split:
        steps = jnp.exp(jax.random.uniform(jax.random.fold_in(own, axis_at), (blocks,), jnp.float32, smallest / len(split), top_value / len(split)))
        gain = gain * jnp.repeat(steps, shape[axis_at] // blocks).reshape([-1 if axis == axis_at else 1 for axis in range(len(shape))])
    return gain


def bell_draw(own_key, shape, deviation, most, cuts=(), held_as=jnp.bfloat16):
    loudness = steps_of(own_key, shape, cuts, -0.22, 0.18) if cuts else 1.0
    array = jax.random.normal(own_key, shape, jnp.float32) * deviation * loudness
    return jnp.minimum(jnp.maximum(array, -most), most).astype(held_as)


def setup_inputs(seed: int = 0) -> dict:
    keys = jax.random.split(jax.random.key(seed), 8)
    zonal_wind = bell_draw(keys[0], (NLAT, LEV, LON), 1.0, 6.0, ((0, 8), (2, 4)), jnp.float32)
    merid_wind = bell_draw(keys[1], (NLAT, LEV, LON), 1.0, 6.0, ((0, 8), (2, 4)), jnp.float32)
    pressure = bell_draw(keys[2], (NLAT, LEV, LON), 1.0, 6.0, ((0, 8), (2, 4)), jnp.float32)
    zonal_metric = jnp.clip(jnp.exp(math.log(1.0) - 1.609438 * jax.random.uniform(keys[3], (NLAT,), jnp.float32) ** steps_of(keys[3], (NLAT,), ((0, 8),), -0.2, 0.2)), 0.2, 1.0)
    helm_inverse = draw_helm_inverse(jax.random.fold_in(keys[7], 71), 0)
    kernel_taps = jnp.clip(jnp.exp(jax.random.uniform(keys[5], (2 * ROWS, KW), jnp.float32, math.log(0.05), math.log(1.0))), 0.05, 1.0)
    filter_width = plant(jax.random.randint(keys[6], (2 * ROWS,), max(1, HALF // 16), HALF + 1), jax.random.fold_in(keys[6], 1), max(1, HALF // 16), HALF).astype(jnp.int32)
    return {"zonal_wind": zonal_wind, "merid_wind": merid_wind, "pressure": pressure, "zonal_metric": zonal_metric, "helm_inverse": helm_inverse, "kernel_taps": kernel_taps, "filter_width": filter_width}


meridional = 0.5
compress = 0.5


def kernels(kernel_taps, filter_width):
    tap_count = kernel_taps.shape[1]
    offsets = jnp.abs(jnp.arange(tap_count, dtype=jnp.int32) - tap_count // 2)
    kept_taps = jnp.where(offsets[None, :] <= filter_width[:, None], kernel_taps, jnp.zeros_like(kernel_taps))
    return kept_taps / jnp.sum(kept_taps, axis=1, keepdims=True)


def filter_polar(values, weights):
    lon_total = values.shape[-1]
    tap_count = weights.shape[1]
    half_span = tap_count // 2
    reversed_taps = weights[:, ::-1]
    padded = jnp.concatenate([reversed_taps, jnp.zeros((weights.shape[0], lon_total - tap_count), weights.dtype)], axis=1)
    kernel_full = jnp.roll(padded, -(tap_count - 1 - half_span), axis=1)
    spectrum = jnp.fft.rfft(values, axis=-1) * jnp.fft.rfft(kernel_full, axis=-1)[:, None, :]
    return jnp.fft.irfft(spectrum, n=lon_total, axis=-1).astype(values.dtype)


def lon_difference(values):
    return 0.5 * (jnp.roll(values, -1, axis=2) - jnp.roll(values, 1, axis=2))


def lat_pair(values, sign_flip):
    lon_total = values.shape[2]
    edges = jnp.stack([values[0], values[-1]])
    partner = jnp.roll(edges, lon_total // 2, axis=2)
    south_rows = jnp.concatenate([sign_flip * partner[:1], values[:-1]], axis=0)
    north_rows = jnp.concatenate([values[1:], sign_flip * partner[1:]], axis=0)
    return south_rows, north_rows


def reference(zonal_wind, merid_wind, pressure, zonal_metric, helm_inverse, kernel_taps, filter_width):
    weights = kernels(kernel_taps, filter_width)
    metric = zonal_metric[:, None, None]
    for step_index in range(2):
        south_rows, north_rows = lat_pair(pressure, 1.0)
        tend_u = -metric * lon_difference(pressure)
        tend_v = -meridional * 0.5 * (north_rows - south_rows)
        tendency = jnp.concatenate([tend_u, tend_v], axis=1)
        polar_rows = jnp.concatenate([tendency[:ROWS], tendency[NLAT - ROWS:]], axis=0)
        smoothed = filter_polar(polar_rows, weights)
        tendency = jnp.concatenate([smoothed[:ROWS], tendency[ROWS:NLAT - ROWS], smoothed[ROWS:]], axis=0)
        zonal_wind = zonal_wind + tendency[:, :LEV]
        merid_wind = merid_wind + tendency[:, LEV:]
        south_rows, north_rows = lat_pair(merid_wind, -1.0)
        divergence = metric * lon_difference(zonal_wind) + meridional * 0.5 * (north_rows - south_rows)
        source = pressure - compress * divergence
        pressure = jnp.einsum("rkl,rlc->rkc", helm_inverse, source, precision=lax.Precision.HIGHEST)
    return zonal_wind, merid_wind, pressure
```

```python
import jax
import jax.numpy as jnp
from jax import lax
from jax.sharding import PartitionSpec as P

meridional = 0.5
compress = 0.5
BLOCK = 256


def kernels(kernel_taps, filter_width):
    tap_count = kernel_taps.shape[1]
    offsets = jnp.abs(jnp.arange(tap_count, dtype=jnp.int32) - tap_count // 2)
    kept_taps = jnp.where(
        offsets[None, :] <= filter_width[:, None], kernel_taps, jnp.zeros_like(kernel_taps)
    )
    return kept_taps / jnp.sum(kept_taps, axis=1, keepdims=True)


def toeplitz(weights, outputs):
    rows, taps = weights.shape
    padded = jnp.concatenate([weights, jnp.zeros((rows, outputs + 1), weights.dtype)], axis=1)
    tiled = jnp.tile(padded, (1, outputs))[:, : outputs * (outputs + taps)]
    return tiled.reshape(rows, outputs, outputs + taps)


def pole_rows(values, sign_flip):
    lat_index, lat_count = lax.axis_index("lat"), lax.axis_size("lat")
    lon_count = lax.axis_size("lon")
    up = [(i, i + 1) for i in range(lat_count - 1)]
    south = lax.ppermute(values[-1], "lat", up)
    north = lax.ppermute(values[0], "lat", [(j, i) for i, j in up])
    route = []
    for lat in (0, lat_count - 1):
        for lon in range(lon_count):
            route.append((lat * lon_count + lon, lat * lon_count + (lon + lon_count // 2) % lon_count))
    edge = jnp.where(lat_index == 0, values[0], values[-1])
    partner = sign_flip * lax.ppermute(edge, ("lat", "lon"), route)
    south = jnp.where(lat_index == 0, partner, south)
    north = jnp.where(lat_index == lat_count - 1, partner, north)
    return south[None], north[None]


def lon_sides(values, width):
    count = lax.axis_size("lon")
    up = [(i, (i + 1) % count) for i in range(count)]
    before = lax.ppermute(values[..., -width:], "lon", up)
    after = lax.ppermute(values[..., :width], "lon", [(j, i) for i, j in up])
    return before, after


def on_device(zonal, merid, pressure, zonal_metric, helm_inverse, kernel_taps, filter_width):
    rows, levels, cols = pressure.shape
    taps = kernel_taps.shape[1]
    half = taps // 2
    lat_index, lat_count = lax.axis_index("lat"), lax.axis_size("lat")
    polar = (lat_index == 0) | (lat_index == lat_count - 1)
    weights = kernels(kernel_taps, filter_width)
    weights = jnp.where(lat_index == 0, weights[:rows], weights[rows:])
    band = toeplitz(weights, BLOCK)
    blocks = -(-cols // BLOCK)
    metric = zonal_metric[:, None, None]
    for step_index in range(2):
        south, north = pole_rows(pressure, 1.0)
        tall = jnp.concatenate([south, pressure, north], axis=0)
        before, after = lon_sides(tall, half + 1)
        wide = jnp.concatenate([before, tall, after], axis=2)
        tend_u = -metric * 0.5 * (wide[1:-1, :, 2:] - wide[1:-1, :, :-2])
        tend_v = -meridional * 0.5 * (wide[2:, :, 1:-1] - wide[:-2, :, 1:-1])
        tendency = jnp.concatenate([tend_u, tend_v], axis=1)
        padded = jnp.pad(tendency, ((0, 0), (0, 0), (0, blocks * BLOCK - cols)))
        windows = jnp.stack(
            [padded[..., b * BLOCK : b * BLOCK + BLOCK + taps] for b in range(blocks)], axis=1
        )
        smooth = jnp.einsum("rbvk,rok->rvbo", windows, band, precision=lax.Precision.HIGH)
        smooth = smooth.reshape(rows, 2 * levels, blocks * BLOCK)[..., :cols]
        smooth = jnp.where(polar, smooth, tendency[..., half : half + cols])
        zonal = zonal + smooth[:, :levels]
        merid = merid + smooth[:, levels:]
        south, north = pole_rows(merid, -1.0)
        before, after = lon_sides(zonal, 1)
        wide = jnp.concatenate([before, zonal, after], axis=2)
        tall = jnp.concatenate([south, merid, north], axis=0)
        divergence = metric * 0.5 * (wide[..., 2:] - wide[..., :-2]) + meridional * 0.5 * (
            tall[2:] - tall[:-2]
        )
        source = pressure - compress * divergence
        pressure = jnp.einsum(
            "rkl,rlc->rkc", helm_inverse, source, precision=lax.Precision.HIGH
        )
    return (zonal, merid, pressure)


def solution(mesh):
    field = P("lat", None, "lon")
    return jax.shard_map(
        on_device,
        mesh=mesh,
        in_specs=(field, field, field, P("lat"), P("lat", None, None), P(), P()),
        out_specs=(field, field, field),
        check_vma=False,
    )
```

```python
import functools

import jax
import jax.numpy as jnp
from jax import lax
from jax.experimental import pallas as pl
from jax.experimental.pallas import tpu as pltpu
from jax.sharding import PartitionSpec as P

meridional = 0.5
compress = 0.5
BLOCK = 256
MESH = pl.DeviceIdType.MESH
NT = (((1,), (1,)), ((), ()))
EXACT = lax.Precision.HIGHEST
SOUTH, NORTH, COL_E, COL_W, WIDE_W, WIDE_E, RIM_W0, RIM_E0, RIM_W9, RIM_E9 = range(10)


def kernels(kernel_taps, filter_width):
    tap_count = kernel_taps.shape[1]
    offsets = jnp.abs(jnp.arange(tap_count, dtype=jnp.int32) - tap_count // 2)
    kept_taps = jnp.where(
        offsets[None, :] <= filter_width[:, None], kernel_taps, jnp.zeros_like(kernel_taps)
    )
    return kept_taps / jnp.sum(kept_taps, axis=1, keepdims=True)


def split(value):
    high = value.astype(jnp.bfloat16)
    return high, (value - high.astype(jnp.float32)).astype(jnp.bfloat16)


def kernel(
    sizes, u_in, v_in, p_in, metric_ref, helm_ref, weight_ref, u_out, v_out, p_out,
    p_tall, v_tall, u_wide, west, east, stage, cols_e, cols_w, send_cols, band_h, band_l,
    send_sem, recv_sem,
):
    rows, levels, cols, half, lats, lons = sizes
    padded = -(-cols // 128) * 128
    lat, lon = lax.axis_index("lat"), lax.axis_index("lon")
    first, final = lat == 0, lat == lats - 1
    polar = jnp.logical_or(first, final)
    inner = jnp.logical_not(polar)
    beside = jnp.logical_or(lat == 1, lat == lats - 2)
    pole = jnp.where(lat == 1, 0, lats - 1)
    shift = lambda n: lax.rem(lon + n + lons, lons)
    across = lons // 2
    last_base = (cols // 128) * 128
    rem = cols - last_base

    barrier = pltpu.get_barrier_semaphore()

    def greet(device):
        pl.semaphore_signal(barrier, inc=1, device_id=device, device_id_type=MESH)

    greet((lat, shift(1)))
    greet((lat, shift(-1)))

    @pl.when(lat > 0)
    def _():
        greet((lat - 1, lon))

    @pl.when(lat < lats - 1)
    def _():
        greet((lat + 1, lon))

    @pl.when(polar)
    def _():
        inward = jnp.where(first, 1, lats - 2)
        greet((inward, shift(1)))
        greet((inward, shift(-1)))
        greet((lat, shift(across)))
        greet((lat, shift(across + 1)))
        greet((lat, shift(across - 1)))

    @pl.when(beside)
    def _():
        greet((pole, shift(1)))
        greet((pole, shift(-1)))

    def fill(r, carry):
        p_tall[0, r + 1, :, 0:cols] = p_in[r]
        return carry

    lax.fori_loop(0, rows, fill, 0)

    @pl.when(polar)
    def _():
        pl.semaphore_wait(barrier, 8)

    @pl.when(jnp.logical_and(inner, beside))
    def _():
        pl.semaphore_wait(barrier, 6)

    @pl.when(jnp.logical_and(inner, jnp.logical_not(beside)))
    def _():
        pl.semaphore_wait(barrier, 4)

    def copy(phase, kind, src, dst, device):
        return pltpu.make_async_remote_copy(
            src_ref=src, dst_ref=dst, send_sem=send_sem.at[phase, kind],
            recv_sem=recv_sem.at[phase, kind], device_id=device, device_id_type=MESH,
        )


    def tall_rows(phase, tall, act):
        up = copy(phase, SOUTH, tall.at[rows], tall.at[0], (lat + 1, lon))
        down = copy(phase, NORTH, tall.at[1], tall.at[rows + 1], (lat - 1, lon))
        over0 = copy(phase, RIM_W0 + 4, tall.at[1], tall.at[0], (lat, shift(across)))
        over9 = copy(phase, RIM_W0 + 4, tall.at[rows], tall.at[rows + 1], (lat, shift(across)))
        if act == "start":
            pl.when(first)(over0.start)
            pl.when(final)(over9.start)
            pl.when(lat < lats - 1)(up.start)
            pl.when(lat > 0)(down.start)
        elif act == "recv":
            pl.when(first)(over0.wait_recv)
            pl.when(final)(over9.wait_recv)
            pl.when(lat > 0)(up.wait_recv)
            pl.when(lat < lats - 1)(down.wait_recv)
        else:
            pl.when(first)(over0.wait_send)
            pl.when(final)(over9.wait_send)
            pl.when(lat < lats - 1)(up.wait_send)
            pl.when(lat > 0)(down.wait_send)

    def columns(phase, act):
        down = copy(phase, COL_E, send_cols.at[phase, 0], cols_e.at[phase], (lat, shift(-1)))
        up = copy(phase, COL_W, send_cols.at[phase, 1], cols_w.at[phase], (lat, shift(1)))
        for one in (down, up):
            if act == "start":
                one.start()
            elif act == "recv":
                one.wait_recv()
            else:
                one.wait_send()

    def wide_sides(step, act):
        phase = 2 * step
        tall = p_tall.at[step]
        side = stage.at[step]

        @pl.when(polar)
        def _():
            up = copy(phase, WIDE_W, side, west.at[step, pl.ds(1, rows)], (lat, shift(1)))
            down = copy(
                phase, WIDE_E, tall.at[pl.ds(1, rows), :, pl.ds(0, half)],
                east.at[step, pl.ds(1, rows)], (lat, shift(-1)),
            )
            for one in (up, down):
                if act == "start":
                    one.start()
                elif act == "recv":
                    one.wait_recv()
                else:
                    one.wait_send()

        def rims(row, slot, kind, lat_to, lon_w, lon_e):
            to_west = copy(
                phase, kind, side.at[row], west.at[step, slot], (lat_to, lon_w)
            )
            to_east = copy(
                phase, kind + 1, tall.at[row + 1, :, pl.ds(0, half)],
                east.at[step, slot], (lat_to, lon_e),
            )
            return to_west, to_east

        def run(pair):
            for one in pair:
                if act == "start":
                    one.start()
                elif act == "recv":
                    one.wait_recv()
                else:
                    one.wait_send()

        own0 = rims(0, 0, RIM_W0, lat, shift(1 - across), shift(-1 - across))
        own9 = rims(rows - 1, rows + 1, RIM_W9, lat, shift(1 - across), shift(-1 - across))
        to_first = rims(0, rows + 1, RIM_W9, 0, shift(1), shift(-1))
        to_final = rims(rows - 1, 0, RIM_W0, lats - 1, shift(1), shift(-1))
        if act == "recv":
            @pl.when(polar)
            def _():
                run(own0)
                run(own9)
        else:
            pl.when(first)(lambda: run(own0))
            pl.when(final)(lambda: run(own9))
            pl.when(lat == 1)(lambda: run(to_first))
            pl.when(lat == lats - 2)(lambda: run(to_final))

    lane = lax.broadcasted_iota(jnp.int32, (rows, 128), 1)
    sub = lax.broadcasted_iota(jnp.int32, (rows, 128), 0)
    lane_l = lax.broadcasted_iota(jnp.int32, (levels, 128), 1)

    def column_of(tile_of, at):
        total = jnp.zeros((rows, levels), jnp.float32)
        base = (at // 128) * 128
        for r in range(rows):
            pick = jnp.where(jnp.logical_and(lane == at - base, sub == r), 1.0, 0.0)
            tile = tile_of(r, base)
            if base == last_base:
                tile = jnp.where(lane_l < rem, tile, 0.0)
            total += lax.dot_general(
                pick, tile, NT, precision=EXACT, preferred_element_type=jnp.float32
            )
        return total

    eye = jnp.where(
        lax.broadcasted_iota(jnp.int32, (levels, levels), 0)
        == lax.broadcasted_iota(jnp.int32, (levels, levels), 1),
        1.0, 0.0,
    )
    row_lane = lax.broadcasted_iota(jnp.int32, (levels, rows), 1)

    def upright(block):
        return lax.dot_general(
            eye, block, NT, precision=EXACT, preferred_element_type=jnp.float32
        )

    def take(stood, r):
        return jnp.sum(jnp.where(row_lane == r, stood, 0.0), axis=1, keepdims=True)

    lane_p = lax.broadcasted_iota(jnp.int32, (levels, padded), 1)
    blocks = -(-cols // BLOCK)
    window = blocks * BLOCK + 2 * half
    lane_w = lax.broadcasted_iota(jnp.int32, (levels, window), 1)
    lane_t = lax.broadcasted_iota(jnp.int32, (levels, half + 128), 1)

    def lon_difference(value, before, after):
        right = jnp.where(lane_p == cols - 1, after, pltpu.roll(value, padded - 1, 1))
        left = jnp.where(lane_p == 0, before, pltpu.roll(value, 1, 1))
        return 0.5 * (right - left)

    def wide_row(step, r):
        own = p_tall[step, r]
        tail = jnp.concatenate(
            [own[:, last_base:padded], jnp.zeros((levels, half), jnp.float32)], axis=1
        )
        moved = jnp.concatenate(
            [east[step, r], jnp.zeros((levels, 128), jnp.float32)], axis=1
        )
        tail = jnp.where(lane_t < rem, tail, pltpu.roll(moved, rem, 1))
        pieces = [west[step, r], own[:, 0:last_base], tail]
        rest = window - half - last_base - half - 128
        if rest:
            pieces.append(jnp.zeros((levels, rest), jnp.float32))
        return jnp.concatenate(pieces, axis=1)

    def send_pressure(step):
        phase = 2 * step
        tall_rows(phase, p_tall.at[step], "start")

        @pl.when(jnp.logical_or(polar, beside))
        def _():
            def edge(r, carry):
                value = p_tall[step, r + 1, :, padded - half - 128 : padded]
                turned = pltpu.roll(value, (half + 128) - (128 - (padded - cols)), 1)
                stage[step, r] = turned[:, 0:half]
                return carry

            lax.fori_loop(0, rows, edge, 0)

        wide_sides(step, "start")
        tile_of = lambda r, base: p_tall[step, r + 1, :, base : base + 128]
        send_cols[phase, 0] = column_of(tile_of, 0)

        @pl.when(polar)
        def _():
            send_cols[phase, 1] = column_of(tile_of, cols - half - 1)

        @pl.when(inner)
        def _():
            send_cols[phase, 1] = column_of(tile_of, cols - 1)

        columns(phase, "start")

    def store_winds(step, r, add_u, add_v, base, width):
        at = slice(base, base + width)
        if step == 0:
            u_wide[r, :, at] = u_in[r, :, at] + add_u
            v_tall[0, r + 1, :, at] = v_in[r, :, at] + add_v
        else:
            u_out[r, :, at] = u_wide[r, :, at] + add_u
            v_tall[1, r + 1, :, at] = v_tall[0, r + 1, :, at] + add_v

    for step in range(2):
        phase = 2 * step
        send_pressure(step)
        if step == 0:
            @pl.when(polar)
            def _():
                def build(r, carry):
                    line = jnp.broadcast_to(
                        weight_ref[pl.ds(r, 1), :], (BLOCK, 2 * half + BLOCK)
                    )
                    matrix = pltpu.roll(line, 0, 1, stride=1, stride_axis=0)
                    band_h[r], band_l[r] = split(matrix)
                    return carry

                lax.fori_loop(0, rows, build, 0)

        tall_rows(phase, p_tall.at[step], "recv")
        columns(phase, "recv")

        @pl.when(polar)
        def _():
            wide_sides(step, "recv")
            far = upright(cols_w[phase])

            def smooth(r, carry):
                scale = -0.5 * metric_ref[r]
                own = wide_row(step, r + 1)
                left = jnp.where(lane_w == 0, take(far, r), pltpu.roll(own, 1, 1))
                tend_u = scale * (pltpu.roll(own, window - 1, 1) - left)
                tend_v = (-meridional * 0.5) * (wide_row(step, r + 2) - wide_row(step, r))
                high, low = split(jnp.concatenate([tend_u, tend_v], axis=0))
                span = BLOCK + 2 * half
                highs = [high[:, b * BLOCK : b * BLOCK + span] for b in range(blocks)]
                lows = [low[:, b * BLOCK : b * BLOCK + span] for b in range(blocks)]
                main = lax.dot_general(
                    jnp.concatenate(highs + lows, axis=0), band_h[r], NT,
                    preferred_element_type=jnp.float32,
                )
                more = lax.dot_general(
                    jnp.concatenate(highs, axis=0), band_l[r], NT,
                    preferred_element_type=jnp.float32,
                )
                tall = 2 * levels
                total = main[: blocks * tall] + main[blocks * tall :] + more
                for b in range(blocks):
                    width = min(BLOCK, cols - b * BLOCK)
                    part = total[b * tall : (b + 1) * tall, :width]
                    store_winds(step, r, part[:levels], part[levels:], b * BLOCK, width)
                return carry

            lax.fori_loop(0, rows, smooth, 0)

        @pl.when(inner)
        def _():
            after, before = upright(cols_e[phase]), upright(cols_w[phase])

            def plain(r, carry):
                change = lon_difference(p_tall[step, r + 1], take(before, r), take(after, r))
                tend_u = -metric_ref[r] * change
                tend_v = (-meridional * 0.5) * (p_tall[step, r + 2] - p_tall[step, r])
                store_winds(step, r, tend_u[:, :cols], tend_v[:, :cols], 0, cols)
                return carry

            lax.fori_loop(0, rows, plain, 0)

        phase = phase + 1
        tall_rows(phase, v_tall.at[step], "start")
        if step == 0:
            tile_of = lambda r, base: u_wide[r, :, base : base + 128]
        else:
            def copy_u(r, carry):
                u_wide[r, :, 0:cols] = u_out[r]
                return carry

            lax.fori_loop(0, rows, copy_u, 0)
            tile_of = lambda r, base: u_wide[r, :, base : base + 128]
        send_cols[phase, 0] = column_of(tile_of, 0)
        send_cols[phase, 1] = column_of(tile_of, cols - 1)
        columns(phase, "start")
        columns(phase, "recv")
        tall_rows(phase, v_tall.at[step], "recv")

        @pl.when(first)
        def _():
            v_tall[step, 0] = -v_tall[step, 0]

        @pl.when(final)
        def _():
            v_tall[step, rows + 1] = -v_tall[step, rows + 1]

        after, before = upright(cols_e[phase]), upright(cols_w[phase])

        def solve(r, carry):
            change = lon_difference(u_wide[r], take(before, r), take(after, r))
            divergence = metric_ref[r] * change + (meridional * 0.5) * (
                v_tall[step, r + 2] - v_tall[step, r]
            )
            source = p_tall[step, r + 1] - compress * divergence
            source = jnp.concatenate(
                [source, jnp.zeros((8, padded), jnp.float32)], axis=0
            )
            high, low = split(source)
            stacked = jnp.concatenate([high, low, high], axis=0)
            result = lax.dot_general(
                helm_ref[r].astype(jnp.bfloat16), stacked, (((1,), (0,)), ((), ())),
                preferred_element_type=jnp.float32,
            )
            if step == 0:
                p_tall[1, r + 1] = result
            else:
                p_out[r] = result[:, :cols]
                v_out[r] = v_tall[1, r + 1, :, 0:cols]
            return carry

        lax.fori_loop(0, rows, solve, 0)

    for step in range(2):
        tall_rows(2 * step, p_tall.at[step], "send")
        wide_sides(step, "send")
        columns(2 * step, "send")
        tall_rows(2 * step + 1, v_tall.at[step], "send")
        columns(2 * step + 1, "send")


def on_device(zonal, merid, pressure, zonal_metric, helm_inverse, kernel_taps, filter_width):
    rows, levels, cols = pressure.shape
    half = kernel_taps.shape[1] // 2
    padded = -(-cols // 128) * 128
    lats, lons = lax.axis_size("lat"), lax.axis_size("lon")
    weights = kernels(kernel_taps, filter_width)
    weights = jnp.where(lax.axis_index("lat") == 0, weights[:rows], weights[rows:])
    weights = jnp.pad(weights, ((0, 0), (0, BLOCK)))
    high = lax.reduce_precision(helm_inverse, 8, 7)
    gap = jnp.zeros((rows, levels, 8), jnp.float32)
    helm = jnp.concatenate([high, gap, high, gap, helm_inverse - high, gap], axis=2)
    sizes = (rows, levels, cols, half, lats, lons)
    vmem = pl.BlockSpec(memory_space=pltpu.VMEM)
    field = jax.ShapeDtypeStruct((rows, levels, cols), jnp.float32)
    return pl.pallas_call(
        functools.partial(kernel, sizes),
        out_shape=(field, field, field),
        in_specs=[vmem, vmem, vmem, pl.BlockSpec(memory_space=pltpu.SMEM), vmem, vmem],
        out_specs=(vmem, vmem, vmem),
        scratch_shapes=[
            pltpu.VMEM((2, rows + 2, levels, padded), jnp.float32),
            pltpu.VMEM((2, rows + 2, levels, padded), jnp.float32),
            pltpu.VMEM((rows, levels, padded), jnp.float32),
            pltpu.VMEM((2, rows + 2, levels, half), jnp.float32),
            pltpu.VMEM((2, rows + 2, levels, half), jnp.float32),
            pltpu.VMEM((2, rows, levels, half), jnp.float32),
            pltpu.VMEM((4, rows, levels), jnp.float32),
            pltpu.VMEM((4, rows, levels), jnp.float32),
            pltpu.VMEM((4, 2, rows, levels), jnp.float32),
            pltpu.VMEM((rows, BLOCK, 2 * half + BLOCK), jnp.bfloat16),
            pltpu.VMEM((rows, BLOCK, 2 * half + BLOCK), jnp.bfloat16),
            pltpu.SemaphoreType.DMA((4, 11)),
            pltpu.SemaphoreType.DMA((4, 11)),
        ],
        compiler_params=pltpu.CompilerParams(
            collective_id=0, has_side_effects=True, vmem_limit_bytes=58 * 1024 * 1024
        ),
    )(zonal, merid, pressure, zonal_metric, helm, weights)


def solution(mesh):
    field = P("lat", None, "lon")
    return jax.shard_map(
        on_device,
        mesh=mesh,
        in_specs=(field, field, field, P("lat"), P("lat", None, None), P(), P()),
        out_specs=(field, field, field),
        check_vma=False,
    )
```

```python
import functools

import jax
import jax.numpy as jnp
from jax import lax
from jax.experimental import pallas as pl
from jax.experimental.pallas import tpu as pltpu
from jax.sharding import PartitionSpec as P

meridional = 0.5
compress = 0.5
BLOCK = 256
MESH = pl.DeviceIdType.MESH
NT = (((1,), (1,)), ((), ()))
EXACT = lax.Precision.HIGHEST
SOUTH, NORTH, COL_E, COL_W, WIDE_W, WIDE_E, RIM_W0, RIM_E0, RIM_W9, RIM_E9 = range(10)
OVER, MID_W, MID_E, TOP_W, TOP_E = range(10, 15)


def split(value):
    high = value.astype(jnp.bfloat16)
    return high, (value - high.astype(jnp.float32)).astype(jnp.bfloat16)


def kernel(
    sizes, u_in, v_in, p_in, metric_ref, helm_ref, taps_ref, width_ref, u_out, v_out, p_out,
    p_tall, v_tall, u_wide, west, east, stage, cols_e, cols_w, send_cols, band_h, band_l,
    send_sem, recv_sem,
):
    rows, levels, cols, half, lats, lons = sizes
    padded = -(-cols // 128) * 128
    lat, lon = lax.axis_index("lat"), lax.axis_index("lon")
    first, final = lat == 0, lat == lats - 1
    polar = jnp.logical_or(first, final)
    inner = jnp.logical_not(polar)
    beside = jnp.logical_or(lat == 1, lat == lats - 2)
    pole = jnp.where(lat == 1, 0, lats - 1)
    shift = lambda n: lax.rem(lon + n + lons, lons)
    across = lons // 2
    last_base = (cols // 128) * 128
    rem = cols - last_base

    barrier = pltpu.get_barrier_semaphore()

    def greet(device):
        pl.semaphore_signal(barrier, inc=1, device_id=device, device_id_type=MESH)

    greet((lat, shift(1)))
    greet((lat, shift(-1)))

    @pl.when(lat > 0)
    def _():
        greet((lat - 1, lon))

    @pl.when(lat < lats - 1)
    def _():
        greet((lat + 1, lon))

    @pl.when(polar)
    def _():
        inward = jnp.where(first, 1, lats - 2)
        greet((inward, shift(1)))
        greet((inward, shift(-1)))
        greet((lat, shift(across)))
        greet((lat, shift(across + 1)))
        greet((lat, shift(across - 1)))

    @pl.when(beside)
    def _():
        greet((pole, shift(1)))
        greet((pole, shift(-1)))

    def fill(r, carry):
        p_tall[0, r + 1, :, 0:cols] = p_in[r]
        return carry

    lax.fori_loop(0, rows, fill, 0)

    @pl.when(polar)
    def _():
        pl.semaphore_wait(barrier, 8)

    @pl.when(jnp.logical_and(inner, beside))
    def _():
        pl.semaphore_wait(barrier, 6)

    @pl.when(jnp.logical_and(inner, jnp.logical_not(beside)))
    def _():
        pl.semaphore_wait(barrier, 4)

    def copy(phase, kind, src, dst, device):
        return pltpu.make_async_remote_copy(
            src_ref=src, dst_ref=dst, send_sem=send_sem.at[phase, kind],
            recv_sem=recv_sem.at[phase, kind], device_id=device, device_id_type=MESH,
        )


    def tall_rows(phase, tall, act):
        up = copy(phase, SOUTH, tall.at[rows], tall.at[0], (lat + 1, lon))
        down = copy(phase, NORTH, tall.at[1], tall.at[rows + 1], (lat - 1, lon))
        over0 = copy(phase, OVER, tall.at[1], tall.at[0], (lat, shift(across)))
        over9 = copy(phase, OVER, tall.at[rows], tall.at[rows + 1], (lat, shift(across)))
        if act == "start":
            pl.when(first)(over0.start)
            pl.when(final)(over9.start)
            pl.when(lat < lats - 1)(up.start)
            pl.when(lat > 0)(down.start)
        elif act == "recv":
            pl.when(first)(over0.wait_recv)
            pl.when(final)(over9.wait_recv)
            pl.when(lat > 0)(up.wait_recv)
            pl.when(lat < lats - 1)(down.wait_recv)
        else:
            pl.when(first)(over0.wait_send)
            pl.when(final)(over9.wait_send)
            pl.when(lat < lats - 1)(up.wait_send)
            pl.when(lat > 0)(down.wait_send)

    def columns(phase, act):
        down = copy(phase, COL_E, send_cols.at[phase, 0], cols_e.at[phase], (lat, shift(-1)))
        up = copy(phase, COL_W, send_cols.at[phase, 1], cols_w.at[phase], (lat, shift(1)))
        for one in (down, up):
            if act == "start":
                one.start()
            elif act == "recv":
                one.wait_recv()
            else:
                one.wait_send()

    def wide_sides(step, act, part=None):
        phase = 2 * step
        tall = p_tall.at[step]
        side = stage.at[step]

        def rims(row, slot, kind, lat_to, lon_w, lon_e):
            to_west = copy(
                phase, kind, side.at[row], west.at[step, slot], (lat_to, lon_w)
            )
            to_east = copy(
                phase, kind + 1, tall.at[row + 1, :, pl.ds(0, half)],
                east.at[step, slot], (lat_to, lon_e),
            )
            return to_west, to_east

        def run(pair):
            for one in pair:
                if act == "start":
                    one.start()
                elif act == "recv":
                    one.wait_recv()
                else:
                    one.wait_send()

        own0 = rims(0, 0, RIM_W0, lat, shift(1 - across), shift(-1 - across))
        own9 = rims(rows - 1, rows + 1, RIM_W9, lat, shift(1 - across), shift(-1 - across))
        to_first = rims(0, rows + 1, RIM_W9, 0, shift(1), shift(-1))
        to_final = rims(rows - 1, 0, RIM_W0, lats - 1, shift(1), shift(-1))

        def chunk(start, count, kind):
            up = copy(
                phase, kind, side.at[pl.ds(start, count)],
                west.at[step, pl.ds(start + 1, count)], (lat, shift(1)),
            )
            down = copy(
                phase, kind + 1, tall.at[pl.ds(start + 1, count), :, pl.ds(0, half)],
                east.at[step, pl.ds(start + 1, count)], (lat, shift(-1)),
            )
            return up, down

        low = chunk(0, 2, WIDE_W)
        high = chunk(rows - 2, 2, TOP_W)
        middle = chunk(2, rows - 4, MID_W)
        if act == "recv":
            if part == "edge":
                run(own0)
                run(own9)
                run(low)
                run(high)
            else:
                run(middle)
        elif part == "middle":
            pl.when(polar)(lambda: run(middle))
        else:
            pl.when(lat == 1)(lambda: run(to_first))
            pl.when(lat == lats - 2)(lambda: run(to_final))
            pl.when(first)(lambda: run(own0))
            pl.when(final)(lambda: run(own9))

            @pl.when(polar)
            def _():
                run(low)
                run(high)

    lane = lax.broadcasted_iota(jnp.int32, (rows, 128), 1)
    sub = lax.broadcasted_iota(jnp.int32, (rows, 128), 0)
    lane_l = lax.broadcasted_iota(jnp.int32, (levels, 128), 1)

    def column_of(tile_of, at):
        total = jnp.zeros((rows, levels), jnp.float32)
        base = (at // 128) * 128
        for r in range(rows):
            pick = jnp.where(jnp.logical_and(lane == at - base, sub == r), 1.0, 0.0)
            tile = tile_of(r, base)
            if base == last_base:
                tile = jnp.where(lane_l < rem, tile, 0.0)
            total += lax.dot_general(
                pick, tile, NT, precision=EXACT, preferred_element_type=jnp.float32
            )
        return total

    eye = jnp.where(
        lax.broadcasted_iota(jnp.int32, (levels, levels), 0)
        == lax.broadcasted_iota(jnp.int32, (levels, levels), 1),
        1.0, 0.0,
    )
    row_lane = lax.broadcasted_iota(jnp.int32, (levels, rows), 1)

    def upright(block):
        return lax.dot_general(
            eye, block, NT, precision=EXACT, preferred_element_type=jnp.float32
        )

    def take(stood, r):
        return jnp.sum(jnp.where(row_lane == r, stood, 0.0), axis=1, keepdims=True)

    lane_p = lax.broadcasted_iota(jnp.int32, (levels, padded), 1)
    blocks = -(-cols // BLOCK)
    window = blocks * BLOCK + 2 * half
    lane_w = lax.broadcasted_iota(jnp.int32, (levels, window), 1)
    lane_t = lax.broadcasted_iota(jnp.int32, (levels, half + 128), 1)

    def lon_difference(value, before, after):
        right = jnp.where(lane_p == cols - 1, after, pltpu.roll(value, padded - 1, 1))
        left = jnp.where(lane_p == 0, before, pltpu.roll(value, 1, 1))
        return 0.5 * (right - left)

    def wide_row(step, r):
        own = p_tall[step, r]
        tail = jnp.concatenate(
            [own[:, last_base:padded], jnp.zeros((levels, half), jnp.float32)], axis=1
        )
        moved = jnp.concatenate(
            [east[step, r], jnp.zeros((levels, 128), jnp.float32)], axis=1
        )
        tail = jnp.where(lane_t < rem, tail, pltpu.roll(moved, rem, 1))
        pieces = [west[step, r], own[:, 0:last_base], tail]
        rest = window - half - last_base - half - 128
        if rest:
            pieces.append(jnp.zeros((levels, rest), jnp.float32))
        return jnp.concatenate(pieces, axis=1)

    def send_pressure(step):
        phase = 2 * step
        tall_rows(phase, p_tall.at[step], "start")

        @pl.when(jnp.logical_or(polar, beside))
        def _():
            def edge(r, carry):
                value = p_tall[step, r + 1, :, padded - half - 128 : padded]
                turned = pltpu.roll(value, (half + 128) - (128 - (padded - cols)), 1)
                stage[step, r] = turned[:, 0:half]
                return carry

            lax.fori_loop(0, rows, edge, 0)

        wide_sides(step, "start", "edge")
        tile_of = lambda r, base: p_tall[step, r + 1, :, base : base + 128]
        send_cols[phase, 0] = column_of(tile_of, 0)

        @pl.when(polar)
        def _():
            send_cols[phase, 1] = column_of(tile_of, cols - half - 1)

        @pl.when(inner)
        def _():
            send_cols[phase, 1] = column_of(tile_of, cols - 1)

        columns(phase, "start")
        wide_sides(step, "start", "middle")

    def store_winds(step, r, add_u, add_v, base, width):
        at = slice(base, base + width)
        if step == 0:
            u_wide[0, r, :, at] = u_in[r, :, at] + add_u
            v_tall[0, r + 1, :, at] = v_in[r, :, at] + add_v
        else:
            u_wide[1, r, :, at] = u_wide[0, r, :, at] + add_u
            v_tall[1, r + 1, :, at] = v_tall[0, r + 1, :, at] + add_v

    for step in range(2):
        phase = 2 * step
        send_pressure(step)
        if step == 0:
            @pl.when(polar)
            def _():
                def build(r, carry):
                    q = r + jnp.where(first, 0, rows)
                    away = jnp.abs(lax.broadcasted_iota(jnp.int32, (1, 2 * half), 1) - half)
                    kept = jnp.where(away <= width_ref[q], taps_ref[pl.ds(q, 1), :], 0.0)
                    kept = kept / jnp.sum(kept, axis=1, keepdims=True)
                    line = jnp.concatenate([kept, jnp.zeros((1, BLOCK), jnp.float32)], axis=1)
                    line = jnp.broadcast_to(line, (BLOCK, 2 * half + BLOCK))
                    matrix = pltpu.roll(line, 0, 1, stride=1, stride_axis=0)
                    band_h[r], band_l[r] = split(matrix)
                    return carry

                lax.fori_loop(0, rows, build, 0)

        columns(phase, "recv")
        tall_rows(phase, p_tall.at[step], "recv")

        @pl.when(polar)
        def _():
            wide_sides(step, "recv", "edge")
            far = upright(cols_w[phase])

            def smooth(r, carry):
                scale = -0.5 * metric_ref[r]
                own = wide_row(step, r + 1)
                left = jnp.where(lane_w == 0, take(far, r), pltpu.roll(own, 1, 1))
                tend_u = scale * (pltpu.roll(own, window - 1, 1) - left)
                tend_v = (-meridional * 0.5) * (wide_row(step, r + 2) - wide_row(step, r))
                high, low = split(jnp.concatenate([tend_u, tend_v], axis=0))
                span = BLOCK + 2 * half
                highs = [high[:, b * BLOCK : b * BLOCK + span] for b in range(blocks)]
                lows = [low[:, b * BLOCK : b * BLOCK + span] for b in range(blocks)]
                main = lax.dot_general(
                    jnp.concatenate(highs + lows, axis=0), band_h[r], NT,
                    preferred_element_type=jnp.float32,
                )
                more = lax.dot_general(
                    jnp.concatenate(highs, axis=0), band_l[r], NT,
                    preferred_element_type=jnp.float32,
                )
                tall = 2 * levels
                total = main[: blocks * tall] + main[blocks * tall :] + more
                for b in range(blocks):
                    width = min(BLOCK, cols - b * BLOCK)
                    part = total[b * tall : (b + 1) * tall, :width]
                    store_winds(step, r, part[:levels], part[levels:], b * BLOCK, width)
                return carry

            lax.fori_loop(0, 2, lambda i, c: smooth(i * (rows - 1), c), 0)
            tall_rows(phase + 1, v_tall.at[step], "start")
            wide_sides(step, "recv", "middle")
            lax.fori_loop(1, rows - 1, smooth, 0)

        @pl.when(inner)
        def _():
            after, before = upright(cols_e[phase]), upright(cols_w[phase])

            def plain(r, carry):
                change = lon_difference(p_tall[step, r + 1], take(before, r), take(after, r))
                tend_u = -metric_ref[r] * change
                tend_v = (-meridional * 0.5) * (p_tall[step, r + 2] - p_tall[step, r])
                store_winds(step, r, tend_u[:, :cols], tend_v[:, :cols], 0, cols)
                return carry

            lax.fori_loop(0, 2, lambda i, c: plain(i * (rows - 1), c), 0)
            tall_rows(phase + 1, v_tall.at[step], "start")
            lax.fori_loop(1, rows - 1, plain, 0)

        phase = phase + 1
        tile_of = lambda r, base: u_wide[step, r, :, base : base + 128]
        send_cols[phase, 0] = column_of(tile_of, 0)
        send_cols[phase, 1] = column_of(tile_of, cols - 1)
        columns(phase, "start")
        columns(phase, "recv")
        after, before = upright(cols_e[phase]), upright(cols_w[phase])

        def solve(r, carry):
            change = lon_difference(u_wide[step, r], take(before, r), take(after, r))
            divergence = metric_ref[r] * change + (meridional * 0.5) * (
                v_tall[step, r + 2] - v_tall[step, r]
            )
            source = p_tall[step, r + 1] - compress * divergence
            high, low = split(source)
            inverse = helm_ref[r]
            inverse_high = inverse.astype(jnp.bfloat16).astype(jnp.float32)
            both = jnp.concatenate([inverse_high, inverse - inverse_high], axis=0)
            product = lax.dot_general(
                both.astype(jnp.bfloat16), jnp.concatenate([high, low], axis=1),
                (((1,), (0,)), ((), ())), preferred_element_type=jnp.float32,
            )
            result = product[:levels, :padded] + product[:levels, padded:]
            result = result + product[levels:, :padded]
            if step == 0:
                p_tall[1, r + 1] = result
            else:
                p_out[r] = result[:, :cols]
                v_out[r] = v_tall[1, r + 1, :, 0:cols]
                u_out[r] = u_wide[1, r, :, 0:cols]
            return carry

        lax.fori_loop(1, rows - 1, solve, 0)
        tall_rows(phase, v_tall.at[step], "recv")

        @pl.when(first)
        def _():
            v_tall[step, 0] = -v_tall[step, 0]

        @pl.when(final)
        def _():
            v_tall[step, rows + 1] = -v_tall[step, rows + 1]

        lax.fori_loop(0, 2, lambda i, c: solve(i * (rows - 1), c), 0)

    for step in range(2):
        tall_rows(2 * step, p_tall.at[step], "send")
        wide_sides(step, "send", "edge")
        wide_sides(step, "send", "middle")
        columns(2 * step, "send")
        tall_rows(2 * step + 1, v_tall.at[step], "send")
        columns(2 * step + 1, "send")


def on_device(zonal, merid, pressure, zonal_metric, helm_inverse, kernel_taps, filter_width):
    rows, levels, cols = pressure.shape
    half = kernel_taps.shape[1] // 2
    padded = -(-cols // 128) * 128
    lats, lons = lax.axis_size("lat"), lax.axis_size("lon")
    sizes = (rows, levels, cols, half, lats, lons)
    smem = pl.BlockSpec(memory_space=pltpu.SMEM)
    vmem = pl.BlockSpec(memory_space=pltpu.VMEM)
    field = jax.ShapeDtypeStruct((rows, levels, cols), jnp.float32)
    return pl.pallas_call(
        functools.partial(kernel, sizes),
        out_shape=(field, field, field),
        in_specs=[vmem, vmem, vmem, smem, vmem, vmem, smem],
        out_specs=(vmem, vmem, vmem),
        scratch_shapes=[
            pltpu.VMEM((2, rows + 2, levels, padded), jnp.float32),
            pltpu.VMEM((2, rows + 2, levels, padded), jnp.float32),
            pltpu.VMEM((2, rows, levels, padded), jnp.float32),
            pltpu.VMEM((2, rows + 2, levels, half), jnp.float32),
            pltpu.VMEM((2, rows + 2, levels, half), jnp.float32),
            pltpu.VMEM((2, rows, levels, half), jnp.float32),
            pltpu.VMEM((4, rows, levels), jnp.float32),
            pltpu.VMEM((4, rows, levels), jnp.float32),
            pltpu.VMEM((4, 2, rows, levels), jnp.float32),
            pltpu.VMEM((rows, BLOCK, 2 * half + BLOCK), jnp.bfloat16),
            pltpu.VMEM((rows, BLOCK, 2 * half + BLOCK), jnp.bfloat16),
            pltpu.SemaphoreType.DMA((4, 15)),
            pltpu.SemaphoreType.DMA((4, 15)),
        ],
        compiler_params=pltpu.CompilerParams(
            collective_id=0, has_side_effects=True, vmem_limit_bytes=58 * 1024 * 1024
        ),
    )(zonal, merid, pressure, zonal_metric, helm_inverse, kernel_taps, filter_width)


def solution(mesh):
    field = P("lat", None, "lon")
    return jax.shard_map(
        on_device,
        mesh=mesh,
        in_specs=(field, field, field, P("lat"), P("lat", None, None), P(), P()),
        out_specs=(field, field, field),
        check_vma=False,
    )
```

```python
import functools

import jax
import jax.numpy as jnp
from jax import lax
from jax.experimental import pallas as pl
from jax.experimental.pallas import tpu as pltpu
from jax.sharding import PartitionSpec as P

meridional = 0.5
compress = 0.5
BLOCK = 256
MESH = pl.DeviceIdType.MESH
NT = (((1,), (1,)), ((), ()))
EXACT = lax.Precision.HIGHEST
SOUTH, NORTH, COL_E, COL_W, WIDE_W, WIDE_E, RIM_W0, RIM_E0, RIM_W9, RIM_E9 = range(10)
OVER, TOP_W, TOP_E, MIDDLE = range(10, 14)


def split(value):
    high = value.astype(jnp.bfloat16)
    return high, (value - high.astype(jnp.float32)).astype(jnp.bfloat16)


def kernel(
    sizes, u_in, v_in, p_in, metric_ref, helm_ref, taps_ref, width_ref, u_out, v_out, p_out,
    p_tall, v_tall, u_wide, west, east, stage, cols_e, cols_w, send_cols, band_h, band_l,
    send_sem, recv_sem,
):
    rows, levels, cols, half, lats, lons = sizes
    padded = -(-cols // 128) * 128
    lat, lon = lax.axis_index("lat"), lax.axis_index("lon")
    first, final = lat == 0, lat == lats - 1
    polar = jnp.logical_or(first, final)
    inner = jnp.logical_not(polar)
    beside = jnp.logical_or(lat == 1, lat == lats - 2)
    pole = jnp.where(lat == 1, 0, lats - 1)
    shift = lambda n: lax.rem(lon + n + lons, lons)
    across = lons // 2
    last_base = (cols // 128) * 128
    rem = cols - last_base

    barrier = pltpu.get_barrier_semaphore()

    def greet(device):
        pl.semaphore_signal(barrier, inc=1, device_id=device, device_id_type=MESH)

    greet((lat, shift(1)))
    greet((lat, shift(-1)))

    @pl.when(lat > 0)
    def _():
        greet((lat - 1, lon))

    @pl.when(lat < lats - 1)
    def _():
        greet((lat + 1, lon))

    @pl.when(polar)
    def _():
        inward = jnp.where(first, 1, lats - 2)
        greet((inward, shift(1)))
        greet((inward, shift(-1)))
        greet((lat, shift(across)))
        greet((lat, shift(across + 1)))
        greet((lat, shift(across - 1)))

    @pl.when(beside)
    def _():
        greet((pole, shift(1)))
        greet((pole, shift(-1)))

    def fill(r, carry):
        p_tall[0, r + 1, :, 0:cols] = p_in[r]
        return carry

    lax.fori_loop(0, rows, fill, 0)

    @pl.when(polar)
    def _():
        pl.semaphore_wait(barrier, 8)

    @pl.when(jnp.logical_and(inner, beside))
    def _():
        pl.semaphore_wait(barrier, 6)

    @pl.when(jnp.logical_and(inner, jnp.logical_not(beside)))
    def _():
        pl.semaphore_wait(barrier, 4)

    def copy(phase, kind, src, dst, device):
        return pltpu.make_async_remote_copy(
            src_ref=src, dst_ref=dst, send_sem=send_sem.at[phase, kind],
            recv_sem=recv_sem.at[phase, kind], device_id=device, device_id_type=MESH,
        )


    def tall_rows(phase, tall, act):
        up = copy(phase, SOUTH, tall.at[rows], tall.at[0], (lat + 1, lon))
        down = copy(phase, NORTH, tall.at[1], tall.at[rows + 1], (lat - 1, lon))
        over0 = copy(phase, OVER, tall.at[1], tall.at[0], (lat, shift(across)))
        over9 = copy(phase, OVER, tall.at[rows], tall.at[rows + 1], (lat, shift(across)))
        if act == "start":
            pl.when(first)(over0.start)
            pl.when(final)(over9.start)
            pl.when(lat < lats - 1)(up.start)
            pl.when(lat > 0)(down.start)
        elif act == "recv":
            pl.when(first)(over0.wait_recv)
            pl.when(final)(over9.wait_recv)
            pl.when(lat > 0)(up.wait_recv)
            pl.when(lat < lats - 1)(down.wait_recv)
        else:
            pl.when(first)(over0.wait_send)
            pl.when(final)(over9.wait_send)
            pl.when(lat < lats - 1)(up.wait_send)
            pl.when(lat > 0)(down.wait_send)

    def columns(phase, act):
        down = copy(phase, COL_E, send_cols.at[phase, 0], cols_e.at[phase], (lat, shift(-1)))
        up = copy(phase, COL_W, send_cols.at[phase, 1], cols_w.at[phase], (lat, shift(1)))
        for one in (down, up):
            if act == "start":
                one.start()
            elif act == "recv":
                one.wait_recv()
            else:
                one.wait_send()

    def wide_sides(step, act, part=None):
        phase = 2 * step
        tall = p_tall.at[step]
        side = stage.at[step]

        def rims(row, slot, kind, lat_to, lon_w, lon_e):
            to_west = copy(
                phase, kind, side.at[row], west.at[step, slot], (lat_to, lon_w)
            )
            to_east = copy(
                phase, kind + 1, tall.at[row + 1, :, pl.ds(0, half)],
                east.at[step, slot], (lat_to, lon_e),
            )
            return to_west, to_east

        def run(pair):
            for one in pair:
                if act == "start":
                    one.start()
                elif act == "recv":
                    one.wait_recv()
                else:
                    one.wait_send()

        own0 = rims(0, 0, RIM_W0, lat, shift(1 - across), shift(-1 - across))
        own9 = rims(rows - 1, rows + 1, RIM_W9, lat, shift(1 - across), shift(-1 - across))
        to_first = rims(0, rows + 1, RIM_W9, 0, shift(1), shift(-1))
        to_final = rims(rows - 1, 0, RIM_W0, lats - 1, shift(1), shift(-1))

        def chunk(start, count, kind):
            up = copy(
                phase, kind, side.at[pl.ds(start, count)],
                west.at[step, pl.ds(start + 1, count)], (lat, shift(1)),
            )
            down = copy(
                phase, kind + 1, tall.at[pl.ds(start + 1, count), :, pl.ds(0, half)],
                east.at[step, pl.ds(start + 1, count)], (lat, shift(-1)),
            )
            return up, down

        low = chunk(0, 2, WIDE_W)
        high = chunk(rows - 2, 2, TOP_W)

        def middle(i, carry):
            run(chunk(2 + i, 1, MIDDLE + 2 * i))
            return carry

        if act == "recv":
            if isinstance(part, str):
                run(own0)
                run(own9)
                run(low)
                run(high)
            else:
                middle(part, 0)
        elif isinstance(part, str) and part == "middle":


            @pl.when(polar)
            def _():
                lax.fori_loop(0, rows - 4, middle, 0)


        else:
            pl.when(lat == 1)(lambda: run(to_first))
            pl.when(lat == lats - 2)(lambda: run(to_final))
            pl.when(first)(lambda: run(own0))
            pl.when(final)(lambda: run(own9))

            @pl.when(polar)
            def _():
                run(low)
                run(high)

    lane = lax.broadcasted_iota(jnp.int32, (rows, 128), 1)
    sub = lax.broadcasted_iota(jnp.int32, (rows, 128), 0)
    lane_l = lax.broadcasted_iota(jnp.int32, (levels, 128), 1)

    def column_of(tile_of, at):
        total = jnp.zeros((rows, levels), jnp.float32)
        base = (at // 128) * 128
        for r in range(rows):
            pick = jnp.where(jnp.logical_and(lane == at - base, sub == r), 1.0, 0.0)
            tile = tile_of(r, base)
            if base == last_base:
                tile = jnp.where(lane_l < rem, tile, 0.0)
            total += lax.dot_general(
                pick, tile, NT, precision=EXACT, preferred_element_type=jnp.float32
            )
        return total

    eye = jnp.where(
        lax.broadcasted_iota(jnp.int32, (levels, levels), 0)
        == lax.broadcasted_iota(jnp.int32, (levels, levels), 1),
        1.0, 0.0,
    )
    row_lane = lax.broadcasted_iota(jnp.int32, (levels, rows), 1)

    def upright(block):
        return lax.dot_general(
            eye, block, NT, precision=EXACT, preferred_element_type=jnp.float32
        )

    def take(stood, r):
        return jnp.sum(jnp.where(row_lane == r, stood, 0.0), axis=1, keepdims=True)

    lane_p = lax.broadcasted_iota(jnp.int32, (levels, padded), 1)
    blocks = -(-cols // BLOCK)
    window = blocks * BLOCK + 2 * half
    lane_w = lax.broadcasted_iota(jnp.int32, (levels, window), 1)
    lane_t = lax.broadcasted_iota(jnp.int32, (levels, half + 128), 1)

    def lon_difference(value, before, after):
        right = jnp.where(lane_p == cols - 1, after, pltpu.roll(value, padded - 1, 1))
        left = jnp.where(lane_p == 0, before, pltpu.roll(value, 1, 1))
        return 0.5 * (right - left)

    def wide_row(step, r):
        own = p_tall[step, r]
        tail = jnp.concatenate(
            [own[:, last_base:padded], jnp.zeros((levels, half), jnp.float32)], axis=1
        )
        moved = jnp.concatenate(
            [east[step, r], jnp.zeros((levels, 128), jnp.float32)], axis=1
        )
        tail = jnp.where(lane_t < rem, tail, pltpu.roll(moved, rem, 1))
        pieces = [west[step, r], own[:, 0:last_base], tail]
        rest = window - half - last_base - half - 128
        if rest:
            pieces.append(jnp.zeros((levels, rest), jnp.float32))
        return jnp.concatenate(pieces, axis=1)

    def send_pressure(step):
        phase = 2 * step
        tall_rows(phase, p_tall.at[step], "start")

        @pl.when(jnp.logical_or(polar, beside))
        def _():
            def edge(r, carry):
                value = p_tall[step, r + 1, :, padded - half - 128 : padded]
                turned = pltpu.roll(value, (half + 128) - (128 - (padded - cols)), 1)
                stage[step, r] = turned[:, 0:half]
                return carry

            lax.fori_loop(0, rows, edge, 0)

        wide_sides(step, "start", "edge")
        tile_of = lambda r, base: p_tall[step, r + 1, :, base : base + 128]
        send_cols[phase, 0] = column_of(tile_of, 0)

        @pl.when(polar)
        def _():
            send_cols[phase, 1] = column_of(tile_of, cols - half - 1)

        @pl.when(inner)
        def _():
            send_cols[phase, 1] = column_of(tile_of, cols - 1)

        columns(phase, "start")
        wide_sides(step, "start", "middle")

    def store_winds(step, r, add_u, add_v, base, width):
        at = slice(base, base + width)
        if step == 0:
            u_wide[0, r, :, at] = u_in[r, :, at] + add_u
            v_tall[0, r + 1, :, at] = v_in[r, :, at] + add_v
        else:
            u_wide[1, r, :, at] = u_wide[0, r, :, at] + add_u
            v_tall[1, r + 1, :, at] = v_tall[0, r + 1, :, at] + add_v

    for step in range(2):
        phase = 2 * step
        send_pressure(step)
        if step == 0:
            @pl.when(polar)
            def _():
                def build(r, carry):
                    q = r + jnp.where(first, 0, rows)
                    away = jnp.abs(lax.broadcasted_iota(jnp.int32, (1, 2 * half), 1) - half)
                    kept = jnp.where(away <= width_ref[q], taps_ref[pl.ds(q, 1), :], 0.0)
                    kept = kept / jnp.sum(kept, axis=1, keepdims=True)
                    line = jnp.concatenate([kept, jnp.zeros((1, BLOCK), jnp.float32)], axis=1)
                    line = jnp.broadcast_to(line, (BLOCK, 2 * half + BLOCK))
                    matrix = pltpu.roll(line, 0, 1, stride=1, stride_axis=0)
                    band_h[r], band_l[r] = split(matrix)
                    return carry

                lax.fori_loop(0, rows, build, 0)

        columns(phase, "recv")
        tall_rows(phase, p_tall.at[step], "recv")

        @pl.when(polar)
        def _():
            wide_sides(step, "recv", "edge")
            far = upright(cols_w[phase])

            def smooth(r, carry):
                scale = -0.5 * metric_ref[r]
                own = wide_row(step, r + 1)
                left = jnp.where(lane_w == 0, take(far, r), pltpu.roll(own, 1, 1))
                tend_u = scale * (pltpu.roll(own, window - 1, 1) - left)
                tend_v = (-meridional * 0.5) * (wide_row(step, r + 2) - wide_row(step, r))
                high, low = split(jnp.concatenate([tend_u, tend_v], axis=0))
                span = BLOCK + 2 * half
                highs = [high[:, b * BLOCK : b * BLOCK + span] for b in range(blocks)]
                lows = [low[:, b * BLOCK : b * BLOCK + span] for b in range(blocks)]
                main = lax.dot_general(
                    jnp.concatenate(highs + lows, axis=0), band_h[r], NT,
                    preferred_element_type=jnp.float32,
                )
                more = lax.dot_general(
                    jnp.concatenate(highs, axis=0), band_l[r], NT,
                    preferred_element_type=jnp.float32,
                )
                tall = 2 * levels
                total = main[: blocks * tall] + main[blocks * tall :] + more
                for b in range(blocks):
                    width = min(BLOCK, cols - b * BLOCK)
                    part = total[b * tall : (b + 1) * tall, :width]
                    store_winds(step, r, part[:levels], part[levels:], b * BLOCK, width)
                return carry

            lax.fori_loop(0, 2, lambda i, c: smooth(i * (rows - 1), c), 0)
            tall_rows(phase + 1, v_tall.at[step], "start")

            def arrive(i, carry):
                wide_sides(step, "recv", i)
                return smooth(i + 1, carry)

            lax.fori_loop(0, rows - 4, arrive, 0)
            lax.fori_loop(rows - 3, rows - 1, smooth, 0)

        @pl.when(inner)
        def _():
            after, before = upright(cols_e[phase]), upright(cols_w[phase])

            def plain(r, carry):
                change = lon_difference(p_tall[step, r + 1], take(before, r), take(after, r))
                tend_u = -metric_ref[r] * change
                tend_v = (-meridional * 0.5) * (p_tall[step, r + 2] - p_tall[step, r])
                store_winds(step, r, tend_u[:, :cols], tend_v[:, :cols], 0, cols)
                return carry

            lax.fori_loop(0, 2, lambda i, c: plain(i * (rows - 1), c), 0)
            tall_rows(phase + 1, v_tall.at[step], "start")
            lax.fori_loop(1, rows - 1, plain, 0)

        phase = phase + 1
        tile_of = lambda r, base: u_wide[step, r, :, base : base + 128]
        send_cols[phase, 0] = column_of(tile_of, 0)
        send_cols[phase, 1] = column_of(tile_of, cols - 1)
        columns(phase, "start")
        columns(phase, "recv")
        after, before = upright(cols_e[phase]), upright(cols_w[phase])

        def solve(r, carry):
            change = lon_difference(u_wide[step, r], take(before, r), take(after, r))
            divergence = metric_ref[r] * change + (meridional * 0.5) * (
                v_tall[step, r + 2] - v_tall[step, r]
            )
            source = p_tall[step, r + 1] - compress * divergence
            high, low = split(source)
            inverse = helm_ref[r]
            inverse_high = inverse.astype(jnp.bfloat16).astype(jnp.float32)
            both = jnp.concatenate([inverse_high, inverse - inverse_high], axis=0)
            product = lax.dot_general(
                both.astype(jnp.bfloat16), jnp.concatenate([high, low], axis=1),
                (((1,), (0,)), ((), ())), preferred_element_type=jnp.float32,
            )
            result = product[:levels, :padded] + product[:levels, padded:]
            result = result + product[levels:, :padded]
            if step == 0:
                p_tall[1, r + 1] = result
            else:
                p_out[r] = result[:, :cols]
                v_out[r] = v_tall[1, r + 1, :, 0:cols]
                u_out[r] = u_wide[1, r, :, 0:cols]
            return carry

        lax.fori_loop(1, rows - 1, solve, 0)
        tall_rows(phase, v_tall.at[step], "recv")

        @pl.when(first)
        def _():
            v_tall[step, 0] = -v_tall[step, 0]

        @pl.when(final)
        def _():
            v_tall[step, rows + 1] = -v_tall[step, rows + 1]

        lax.fori_loop(0, 2, lambda i, c: solve(i * (rows - 1), c), 0)

    for step in range(2):
        tall_rows(2 * step, p_tall.at[step], "send")
        wide_sides(step, "send", "edge")
        wide_sides(step, "send", "middle")
        columns(2 * step, "send")
        tall_rows(2 * step + 1, v_tall.at[step], "send")
        columns(2 * step + 1, "send")


def on_device(zonal, merid, pressure, zonal_metric, helm_inverse, kernel_taps, filter_width):
    rows, levels, cols = pressure.shape
    half = kernel_taps.shape[1] // 2
    padded = -(-cols // 128) * 128
    lats, lons = lax.axis_size("lat"), lax.axis_size("lon")
    sizes = (rows, levels, cols, half, lats, lons)
    smem = pl.BlockSpec(memory_space=pltpu.SMEM)
    vmem = pl.BlockSpec(memory_space=pltpu.VMEM)
    field = jax.ShapeDtypeStruct((rows, levels, cols), jnp.float32)
    return pl.pallas_call(
        functools.partial(kernel, sizes),
        out_shape=(field, field, field),
        in_specs=[vmem, vmem, vmem, smem, vmem, vmem, smem],
        out_specs=(vmem, vmem, vmem),
        scratch_shapes=[
            pltpu.VMEM((2, rows + 2, levels, padded), jnp.float32),
            pltpu.VMEM((2, rows + 2, levels, padded), jnp.float32),
            pltpu.VMEM((2, rows, levels, padded), jnp.float32),
            pltpu.VMEM((2, rows + 2, levels, half), jnp.float32),
            pltpu.VMEM((2, rows + 2, levels, half), jnp.float32),
            pltpu.VMEM((2, rows, levels, half), jnp.float32),
            pltpu.VMEM((4, rows, levels), jnp.float32),
            pltpu.VMEM((4, rows, levels), jnp.float32),
            pltpu.VMEM((4, 2, rows, levels), jnp.float32),
            pltpu.VMEM((rows, BLOCK, 2 * half + BLOCK), jnp.bfloat16),
            pltpu.VMEM((rows, BLOCK, 2 * half + BLOCK), jnp.bfloat16),
            pltpu.SemaphoreType.DMA((4, 5 + 2 * rows)),
            pltpu.SemaphoreType.DMA((4, 5 + 2 * rows)),
        ],
        compiler_params=pltpu.CompilerParams(
            collective_id=0, has_side_effects=True, vmem_limit_bytes=58 * 1024 * 1024
        ),
    )(zonal, merid, pressure, zonal_metric, helm_inverse, kernel_taps, filter_width)


def solution(mesh):
    field = P("lat", None, "lon")
    return jax.shard_map(
        on_device,
        mesh=mesh,
        in_specs=(field, field, field, P("lat"), P("lat", None, None), P(), P()),
        out_specs=(field, field, field),
        check_vma=False,
    )
```
